128 devices in a mesh: ctx: 16 (over x, z), dp: 8 (over y, core).
Axes of the slice: x: 4, y: 4, z: 4, core: 2. Of those that a mesh axis runs over, the one named last changes fastest.
Arguments:
- queries: bfloat16 [8, 2048, 8192], P('dp', 'ctx'), may hold values from -25 to 25
- grad_out: bfloat16 [8, 2048, 8192], P('dp', 'ctx'), may hold values from -6 to 6
- key_raw: bfloat16 [8, 16, 256, 1024], P('dp', 'ctx'), may hold values from -5 to 5
- values: bfloat16 [8, 16, 256, 1024], P('dp', 'ctx'), may hold values from -6 to 6
- key_gain: float32 [128], replicated, may hold values from 0.5 to 1.5
- image_pos: int32 [8, 16], P('dp', 'ctx'), may hold values from 0 to 127, as said below
Outputs:
- grad_queries: bfloat16 [8, 2048, 8192], P('dp', 'ctx')
- grad_key_raw: bfloat16 [8, 16, 256, 1024], P('dp', 'ctx')
- grad_values: bfloat16 [8, 16, 256, 1024], P('dp', 'ctx')
- grad_gain: float32 [128], replicated
The draws below stay inside these ranges and needn't reach their ends.
Inputs may be any that keep to these rules, and one draw needn't show every extreme that they name: `image_pos`: the image of the first shard of each row stands at position 0 and that of the last shard at 127.
All inputs are finite; a program needn't handle non-finite values.
Results may differ from the reference program's by a relative error of at most 0.0054.
The reference program's roundings to bfloat16 on the way count: a program that leaves them out, or rounds other values in their place, can miss the bound.
Values may be sent and summed in bfloat16 or wider, within the bound.
No kernel may reach another device: no remote copies, remote signals or barrier semaphores. Data moves between devices by JAX's collectives and lax.ppermute only.
A program may use at most 320 MiB of HBM per device.

```python
import jax
import jax.numpy as jnp
from jax import lax

HQ = 64
KVH = 8
HD = 128
DOC_IMG = 4
TOK_DEV = 128
MROWS = 256
TOKENS = 2048
N_CTX = 16
N_DP = 8


def draw_queries(key, part):
    key = jax.random.fold_in(key, 11)
    shape = (N_DP, TOKENS, HQ * HD)
    drawn = jax.random.truncated_normal(key, -4.0, 4.0, shape, jnp.float32)
    return drawn.astype(jnp.bfloat16)


def draw_key_raw(key, part):
    key = jax.random.fold_in(key, 12)
    shape = (N_DP, N_CTX, MROWS, KVH * HD)
    drawn = jax.random.truncated_normal(key, -4.0, 4.0, shape, jnp.float32)
    return drawn.astype(jnp.bfloat16)


def draw_image_pos(key, part):
    key = jax.random.fold_in(key, 13)
    drawn = jax.random.randint(key, (N_DP, N_CTX), 0, TOK_DEV)
    column = jnp.arange(N_CTX)[None, :]
    drawn = jnp.where(column == 0, 0, jnp.where(column == N_CTX - 1, TOK_DEV - 1, drawn))
    return drawn.astype(jnp.int32)


def block_levels(key, dims, cuts, low, high):
    def one(position, parts):
        heights = jax.random.uniform(jax.random.fold_in(jax.random.fold_in(key, 6), position), (parts,), jnp.float32, low / len(cuts), high / len(cuts))
        return jnp.repeat(jnp.exp(heights), dims[position] // parts).reshape((-1,) + (1,) * (len(dims) - position - 1))

    loudness = one(*cuts[0])
    for cut in cuts[1:]:
        loudness = loudness * one(*cut)
    return loudness


def scatter_about(key, extent, width, bound, shards=(), held_as=jnp.bfloat16):
    entries = jax.random.normal(key, extent, jnp.float32) * width
    if len(shards) > 0:
        entries = block_levels(key, extent, shards, -0.22, 0.18) * entries
    return jnp.clip(entries, min=-bound, max=bound).astype(held_as)


def setup_inputs(seed: int = 0) -> dict:
    streams_of = jax.random.split(jax.random.key(seed), 7)
    queries = draw_queries(jax.random.fold_in(streams_of[6], 71), 0)
    grad_out = scatter_about(streams_of[1], (N_DP, TOKENS, HQ * HD), 1.0, 6.0, ((0, 8), (1, 16)))
    key_raw = draw_key_raw(jax.random.fold_in(streams_of[6], 71), 0)
    values = scatter_about(streams_of[3], (N_DP, N_CTX, MROWS, KVH * HD), 1.0, 6.0, ((0, 8), (1, 16)))
    key_gain = jnp.clip(1.0 + 0.1 * jax.random.normal(streams_of[4], (HD,), jnp.float32), 0.5, 1.5)
    image_pos = draw_image_pos(jax.random.fold_in(streams_of[6], 71), 0)
    return {"queries": queries, "grad_out": grad_out, "key_raw": key_raw, "values": values, "key_gain": key_gain, "image_pos": image_pos}


def key_norm(key_raw, key_gain):
    shaped = key_raw.astype(jnp.float32).reshape(key_raw.shape[:-1] + (KVH, HD))
    inv_rms = lax.rsqrt(lax.optimization_barrier(jnp.mean(shaped * shaped, -1, keepdims=True)) + 1e-05)
    unit_keys = shaped * inv_rms
    normed = (unit_keys * key_gain).astype(jnp.bfloat16).reshape(key_raw.shape)
    return (lax.optimization_barrier(normed), unit_keys, inv_rms)

def row_pass(operands):
    query_row, grad_row, key_row, value_row, pos_row = operands
    padding = jnp.zeros((DOC_IMG, MROWS, KVH * HD), jnp.bfloat16)
    key_padded = jnp.concatenate([padding, key_row], 0)
    value_padded = jnp.concatenate([padding, value_row], 0)
    span_rows = (DOC_IMG + 1) * MROWS
    scaling = HD ** (-0.5)

    def visit(state, shard_id):
        key_accum, value_accum = state
        start = (shard_id * TOK_DEV).astype(jnp.int32)
        query_block = lax.dynamic_slice_in_dim(query_row, start, TOK_DEV, 0).astype(jnp.float32).reshape(TOK_DEV, KVH, HQ // KVH, HD)
        grad_block = lax.dynamic_slice_in_dim(grad_row, start, TOK_DEV, 0).astype(jnp.float32).reshape(TOK_DEV, KVH, HQ // KVH, HD)
        key_block = lax.dynamic_slice_in_dim(key_padded, shard_id, DOC_IMG + 1, 0).astype(jnp.float32).reshape(span_rows, KVH, HD)
        value_block = lax.dynamic_slice_in_dim(value_padded, shard_id, DOC_IMG + 1, 0).astype(jnp.float32).reshape(span_rows, KVH, HD)
        scores = jnp.einsum('tkgd,rkd->kgtr', query_block, key_block) * scaling
        dprob = jnp.einsum('tkgd,rkd->kgtr', grad_block, value_block)
        tok_index = jnp.arange(TOK_DEV, dtype=jnp.int32)
        last_image = jnp.where(tok_index >= pos_row[shard_id], shard_id, shard_id - 1)
        first_image = last_image // DOC_IMG * DOC_IMG
        image_ids = shard_id - DOC_IMG + jnp.arange(span_rows, dtype=jnp.int32) // MROWS
        visible = (image_ids[None, :] >= first_image[:, None]) & (image_ids[None, :] <= last_image[:, None])
        row_max = lax.optimization_barrier(jnp.max(jnp.where(visible, scores, -1e+30), -1, keepdims=True))
        weights = jnp.where(visible, jnp.exp(scores - row_max), 0.0)
        total = lax.optimization_barrier(jnp.sum(weights, -1, keepdims=True))
        log_total = row_max + jnp.log(total)
        prob = jnp.where(visible, jnp.exp(scores - log_total), 0.0)
        delta = lax.optimization_barrier(jnp.sum(prob * dprob, -1, keepdims=True))
        prob_low = lax.optimization_barrier(prob.astype(jnp.bfloat16)).astype(jnp.float32)
        dscore = lax.optimization_barrier((prob * (dprob - delta)).astype(jnp.bfloat16)).astype(jnp.float32)
        dquery = (scaling * jnp.einsum('kgtr,rkd->tkgd', dscore, key_block)).reshape(TOK_DEV, HQ * HD).astype(jnp.bfloat16)
        dkey = (scaling * jnp.einsum('kgtr,tkgd->rkd', dscore, query_block)).reshape(DOC_IMG + 1, MROWS, KVH * HD)
        dvalue = jnp.einsum('kgtr,tkgd->rkd', prob_low, grad_block).reshape(DOC_IMG + 1, MROWS, KVH * HD)
        key_accum = lax.dynamic_update_slice_in_dim(key_accum, lax.dynamic_slice_in_dim(key_accum, shard_id, DOC_IMG + 1, 0) + dkey, shard_id, 0)
        value_accum = lax.dynamic_update_slice_in_dim(value_accum, lax.dynamic_slice_in_dim(value_accum, shard_id, DOC_IMG + 1, 0) + dvalue, shard_id, 0)
        return ((key_accum, value_accum), dquery)
    empty = jnp.zeros((N_CTX + DOC_IMG, MROWS, KVH * HD), jnp.float32)
    finals, dqueries = lax.scan(visit, (empty, empty), jnp.arange(N_CTX, dtype=jnp.int32))
    return (dqueries.reshape(TOKENS, HQ * HD), finals[0][DOC_IMG:], finals[1][DOC_IMG:])

def reference(queries, grad_out, key_raw, values, key_gain, image_pos):
    normed, unit_keys, inv_rms = key_norm(key_raw, key_gain)
    grad_queries, grad_norm, value_grads = lax.map(row_pass, (queries, grad_out, normed, values, image_pos))
    grad_norm = grad_norm.reshape(unit_keys.shape)
    grad_gain = lax.optimization_barrier(jnp.sum(grad_norm * unit_keys, axis=(0, 1, 2, 3)))
    scaled = grad_norm * key_gain
    grad_key_raw = inv_rms * (scaled - unit_keys * lax.optimization_barrier(jnp.mean(scaled * unit_keys, -1, keepdims=True)))
    grad_key_raw = grad_key_raw.reshape(key_raw.shape).astype(jnp.bfloat16)
    return (grad_queries, grad_key_raw, value_grads.astype(jnp.bfloat16), grad_gain)
```

```python
import functools

import jax
import jax.numpy as jnp
from jax import lax
import jax.experimental.pallas as pl
import jax.experimental.pallas.tpu as pltpu
from jax.sharding import PartitionSpec as P

DOC_IMG = 4
SPAN = DOC_IMG + 1
CHUNKS = 2
HD = 128
MASKED = -1e30
SCALE = HD**-0.5
LOG2E = 1.4426950408889634
NT = (((1,), (1,)), ((), ()))
TN = (((0,), (0,)), ((), ()))
NN = (((1,), (0,)), ((), ()))
VMEM_LIMIT = 40 * 2**20


def dot(left, right, dims):
    return lax.dot_general(left, right, dims, preferred_element_type=jnp.float32)


def unit_norm(raw):
    wide = raw.astype(jnp.float32)
    inv_rms = lax.rsqrt(jnp.mean(wide * wide, -1, keepdims=True) + 1e-05)
    return wide * inv_rms, inv_rms


def pack_kernel(key_ref, value_ref, out_ref):
    for head in range(key_ref.shape[1] // HD):
        left = 2 * HD * head
        out_ref[:, left : left + HD] = key_ref[:, HD * head : HD * (head + 1)]
        out_ref[:, left + HD : left + 2 * HD] = value_ref[:, HD * head : HD * (head + 1)]


def pack(key_raw, values, chunk):
    rows, width = key_raw.shape
    part = width // CHUNKS
    return pl.pallas_call(
        pack_kernel,
        grid=(1,),
        in_specs=[pl.BlockSpec((rows, part), lambda i: (0, chunk))] * 2,
        out_specs=pl.BlockSpec((rows, 2 * part), lambda i: (0, 0)),
        out_shape=jax.ShapeDtypeStruct((rows, 2 * part), key_raw.dtype),
        cost_estimate=pl.CostEstimate(flops=0, bytes_accessed=8 * rows * part, transcendentals=0),
    )(key_raw, values)


def head_work(
    images, meta, q_ref, do_ref, key_ref, value_ref, recv, gain_ref,
    dq_ref, own_k, own_v, parts, gain_part, s_ref, dp_ref, normed, dk_ref, dv_ref,
):
    shard, position = meta[0], meta[1]
    gain = gain_ref[...]
    tokens = q_ref.shape[0]
    group = q_ref.shape[1] // HD
    token = lax.broadcasted_iota(jnp.int32, (1, 2 * tokens), 1) % tokens
    bias = {}
    for i in images:
        raw = key_ref[...] if i == 0 else recv[i - 1][:, :HD]
        normed[i] = (unit_norm(raw)[0] * gain).astype(jnp.bfloat16)
        if i == 0:
            bias[i] = jnp.where(token >= position, 0.0, MASKED)
        elif len(images) == SPAN:
            bias[i] = jnp.where(token < position, 0.0, MASKED)
        else:
            bias[i] = jnp.where(i <= shard, 0.0, MASKED)
    for pair in range(group // 2):
        heads = [2 * pair, 2 * pair + 1]
        q_pair = jnp.concatenate([q_ref[:, g * HD : (g + 1) * HD] for g in heads], 0)
        do_pair = jnp.concatenate([do_ref[:, g * HD : (g + 1) * HD] for g in heads], 0)
        top = None
        for i in images:
            scores = dot(normed[i], q_pair, NT) * (SCALE * LOG2E) + bias[i]
            s_ref[i] = scores
            high = jnp.max(scores, 0, keepdims=True)
            top = high if top is None else jnp.maximum(top, high)
        total = 0.0
        weighted = 0.0
        for i in images:
            value = value_ref[...] if i == 0 else recv[i - 1][:, HD:]
            dprob = dot(value, do_pair, NT)
            weight = jnp.exp2(s_ref[i] - top)
            s_ref[i] = weight
            dp_ref[i] = dprob
            total = total + jnp.sum(weight, 0, keepdims=True)
            weighted = weighted + jnp.sum(weight * dprob, 0, keepdims=True)
        inverse = 1.0 / total
        delta = weighted * inverse
        dq_turned = 0.0
        for i in images:
            prob = s_ref[i] * inverse
            prob_low = prob.astype(jnp.bfloat16)
            dscore = (prob * (dp_ref[i] - delta)).astype(jnp.bfloat16)
            dv = dot(prob_low, do_pair, NN)
            dk = dot(dscore, q_pair, NN)
            if pair == 0:
                dv_ref[i] = dv
                dk_ref[i] = dk
            else:
                dv_ref[i] += dv
                dk_ref[i] += dk
            dq_turned = dq_turned + dot(normed[i], dscore, TN)
        dq = (dq_turned.T * SCALE).astype(jnp.bfloat16)
        for j, g in enumerate(heads):
            dq_ref[:, g * HD : (g + 1) * HD] = dq[j * tokens : (j + 1) * tokens]
    gain_sum = jnp.zeros_like(gain)
    for i in images:
        raw = key_ref[...] if i == 0 else recv[i - 1][:, :HD]
        dk = dk_ref[i] * SCALE
        gain_sum = gain_sum + jnp.sum(dk * unit_norm(raw)[0], 0, keepdims=True)
        if i == 0:
            own_k[...] = dk
            own_v[...] = dv_ref[i]
        else:
            parts[i - 1][:, :HD] = dk.astype(jnp.bfloat16)
            parts[i - 1][:, HD:] = dv_ref[i].astype(jnp.bfloat16)
    gain_part[...] += gain_sum


def attend_kernel(meta, q_ref, do_ref, key_ref, value_ref, *rest, aliased):
    recv, gain_ref, rest = rest[:DOC_IMG], rest[DOC_IMG], rest[DOC_IMG + 1 :]
    if aliased:
        rest = rest[1:]
    dq_ref, own_k, own_v, *rest = rest
    parts, gain_part, scratch = rest[:DOC_IMG], rest[DOC_IMG], rest[DOC_IMG + 1 :]

    @pl.when(pl.program_id(0) == 0)
    def _():
        gain_part[...] = jnp.zeros_like(gain_part)

    args = (
        meta, q_ref, do_ref, key_ref, value_ref, recv, gain_ref,
        dq_ref, own_k, own_v, parts, gain_part, *scratch,
    )

    @pl.when(meta[0] == 0)
    def _():
        head_work(tuple(range(SPAN)), *args)

    @pl.when(meta[0] != 0)
    def _():
        head_work(tuple(range(DOC_IMG)), *args)


def attend(meta, queries, grad_out, key_raw, values, recv, gain, dq, chunk):
    tokens, width = queries.shape
    rows = key_raw.shape[0]
    kv_heads = key_raw.shape[1] // HD
    group = width // HD // kv_heads
    heads = kv_heads // CHUNKS
    first = chunk * heads
    wide = pl.BlockSpec((tokens, group * HD), lambda h: (0, first + h))
    own = pl.BlockSpec((rows, HD), lambda h: (0, first + h))
    part = pl.BlockSpec((rows, 2 * HD), lambda h: (0, h))
    local = pl.BlockSpec((rows, HD), lambda h: (0, h))
    single = pl.BlockSpec((1, HD), lambda h: (0, 0))
    in_specs = [pl.BlockSpec(memory_space=pltpu.SMEM), wide, wide, own, own]
    in_specs += [part] * DOC_IMG + [single]
    args = [meta, queries, grad_out, key_raw, values, *recv, gain]
    aliases = {}
    if dq is not None:
        aliases = {len(args): 0}
        in_specs.append(pl.BlockSpec(memory_space=pl.ANY))
        args.append(dq)
    f32, bf16 = jnp.float32, jnp.bfloat16
    outs = pl.pallas_call(
        functools.partial(attend_kernel, aliased=dq is not None),
        grid=(heads,),
        in_specs=in_specs,
        out_specs=[wide, local, local] + [part] * DOC_IMG + [single],
        out_shape=[jax.ShapeDtypeStruct(queries.shape, bf16)]
        + [jax.ShapeDtypeStruct((rows, heads * HD), f32)] * 2
        + [jax.ShapeDtypeStruct((rows, 2 * heads * HD), bf16)] * DOC_IMG
        + [jax.ShapeDtypeStruct((1, HD), f32)],
        scratch_shapes=[
            pltpu.VMEM((SPAN, rows, 2 * tokens), f32),
            pltpu.VMEM((SPAN, rows, 2 * tokens), f32),
            pltpu.VMEM((SPAN, rows, HD), bf16),
            pltpu.VMEM((SPAN, rows, HD), f32),
            pltpu.VMEM((SPAN, rows, HD), f32),
        ],
        input_output_aliases=aliases,
        compiler_params=pltpu.CompilerParams(vmem_limit_bytes=VMEM_LIMIT),
        cost_estimate=pl.CostEstimate(
            flops=10 * heads * group * tokens * SPAN * rows * HD,
            bytes_accessed=heads * (6 * group * tokens * HD + 24 * SPAN * rows * HD),
            transcendentals=heads * group * tokens * SPAN * rows,
        ),
    )(*args)
    return outs[0], outs[1], outs[2], outs[3 : 3 + DOC_IMG], outs[3 + DOC_IMG]


def finish_kernel(key_ref, own_k, own_v, *rest, aliased):
    back, gain_ref, rest = rest[:DOC_IMG], rest[DOC_IMG], rest[DOC_IMG + 1 :]
    if aliased:
        rest = rest[2:]
    gk_ref, gv_ref = rest
    unit, inv_rms = unit_norm(key_ref[...])
    dk, dv = own_k[...], own_v[...]
    for ref in back:
        dk = dk + ref[:, :HD].astype(jnp.float32)
        dv = dv + ref[:, HD:].astype(jnp.float32)
    scaled = dk * gain_ref[...]
    inner = jnp.mean(scaled * unit, -1, keepdims=True)
    gk_ref[...] = (inv_rms * (scaled - unit * inner)).astype(gk_ref.dtype)
    gv_ref[...] = dv.astype(gv_ref.dtype)


def finish(key_raw, own_k, own_v, back, gain, done, chunk):
    rows, width = key_raw.shape
    heads = width // HD // CHUNKS
    first = chunk * heads
    local = pl.BlockSpec((rows, HD), lambda h: (0, h))
    part = pl.BlockSpec((rows, 2 * HD), lambda h: (0, h))
    placed = pl.BlockSpec((rows, HD), lambda h: (0, first + h))
    args = [key_raw, own_k, own_v, *back, gain]
    in_specs = [placed, local, local] + [part] * DOC_IMG + [pl.BlockSpec((1, HD), lambda h: (0, 0))]
    aliases = {}
    if done is not None:
        aliases = {len(args): 0, len(args) + 1: 1}
        in_specs += [pl.BlockSpec(memory_space=pl.ANY)] * 2
        args += done
    return pl.pallas_call(
        functools.partial(finish_kernel, aliased=done is not None),
        grid=(heads,),
        in_specs=in_specs,
        out_specs=[placed, placed],
        out_shape=[jax.ShapeDtypeStruct(key_raw.shape, jnp.bfloat16)] * 2,
        input_output_aliases=aliases,
        cost_estimate=pl.CostEstimate(
            flops=20 * rows * heads * HD, bytes_accessed=30 * rows * heads * HD, transcendentals=0
        ),
    )(*args)


def reader_pairs(count, distance):
    pairs = []
    for reader in range(distance, count):
        place = reader % DOC_IMG
        if place == 0 or distance <= place:
            pairs.append((reader - distance, reader))
    return pairs


def all_sum(value):
    for axis in ("dp", "ctx"):
        count = lax.axis_size(axis)
        step = 1
        while step < count:
            value = value + lax.ppermute(value, axis, [(i, i ^ step) for i in range(count)])
            step *= 2
    return value


def shards(queries, grad_out, key_raw, values, key_gain, image_pos):
    count = lax.axis_size("ctx")
    queries, grad_out = queries[0], grad_out[0]
    key_raw, values = key_raw[0, 0], values[0, 0]
    gain = key_gain[None]
    meta = jnp.stack([lax.axis_index("ctx") % DOC_IMG, image_pos[0, 0]]).astype(jnp.int32)
    pairs = [reader_pairs(count, distance) for distance in range(1, SPAN)]
    recv = []
    for chunk in range(CHUNKS):
        packed = pack(key_raw, values, chunk)
        recv.append([lax.ppermute(packed, "ctx", to) for to in pairs])
    dq = None
    gain_part = 0.0
    held = []
    for chunk in range(CHUNKS):
        dq, own_k, own_v, parts, part = attend(
            meta, queries, grad_out, key_raw, values, recv[chunk], gain, dq, chunk
        )
        gain_part = gain_part + part
        back = [
            lax.ppermute(value, "ctx", [(reader, owner) for owner, reader in to])
            for value, to in zip(parts, pairs)
        ]
        held.append((own_k, own_v, back))
    grad_gain = all_sum(gain_part)
    done = None
    for chunk, (own_k, own_v, back) in enumerate(held):
        done = finish(key_raw, own_k, own_v, back, gain, done, chunk)
    return dq[None], done[0][None, None], done[1][None, None], grad_gain[0]


def solution(mesh):
    return jax.shard_map(
        shards,
        mesh=mesh,
        in_specs=(
            P("dp", "ctx", None),
            P("dp", "ctx", None),
            P("dp", "ctx", None, None),
            P("dp", "ctx", None, None),
            P(),
            P("dp", "ctx"),
        ),
        out_specs=(
            P("dp", "ctx", None),
            P("dp", "ctx", None, None),
            P("dp", "ctx", None, None),
            P(),
        ),
        check_vma=False,
    )
```

```python
import functools

import jax
import jax.numpy as jnp
from jax import lax
import jax.experimental.pallas as pl
import jax.experimental.pallas.tpu as pltpu
from jax.sharding import PartitionSpec as P

DOC_IMG = 4
SPAN = DOC_IMG + 1
HEADS = (4, 4)
HD = 128
MASKED = -1e30
SCALE = HD**-0.5
LOG2E = 1.4426950408889634
NT = (((1,), (1,)), ((), ()))
TN = (((0,), (0,)), ((), ()))
NN = (((1,), (0,)), ((), ()))
VMEM_LIMIT = 60 * 2**20


def dot(left, right, dims):
    return lax.dot_general(left, right, dims, preferred_element_type=jnp.float32)


def unit_norm(raw):
    wide = raw.astype(jnp.float32)
    inv_rms = lax.rsqrt(jnp.mean(wide * wide, -1, keepdims=True) + 1e-05)
    return wide * inv_rms, inv_rms


def pack_kernel(key_ref, value_ref, out_ref):
    for head in range(key_ref.shape[1] // HD):
        left = 2 * HD * head
        out_ref[:, left : left + HD] = key_ref[:, HD * head : HD * (head + 1)]
        out_ref[:, left + HD : left + 2 * HD] = value_ref[:, HD * head : HD * (head + 1)]


def pack(key_raw, values, chunk):
    rows, width = key_raw.shape
    first, heads = sum(HEADS[:chunk]), HEADS[chunk]
    part = heads * HD
    return pl.pallas_call(
        pack_kernel,
        grid=(heads // 2,),
        in_specs=[pl.BlockSpec((rows, 2 * HD), lambda i: (0, first // 2 + i))] * 2,
        out_specs=pl.BlockSpec((rows, 4 * HD), lambda i: (0, i)),
        out_shape=jax.ShapeDtypeStruct((rows, 2 * part), key_raw.dtype),
        cost_estimate=pl.CostEstimate(flops=0, bytes_accessed=8 * rows * part, transcendentals=0),
    )(key_raw, values)


def head_work(
    images, meta, q_ref, do_ref, key_ref, value_ref, recv, gain_ref,
    dq_ref, own_k, own_v, parts, gain_part, s_ref, dp_ref, normed, dk_ref, dv_ref,
):
    shard, position = meta[0], meta[1]
    gain = gain_ref[...]
    tokens = q_ref.shape[0]
    group = q_ref.shape[1] // HD
    token = lax.broadcasted_iota(jnp.int32, (1, 2 * tokens), 1) % tokens
    bias = {}
    for i in images:
        raw = key_ref[...] if i == 0 else recv[i - 1][:, :HD]
        normed[i] = (unit_norm(raw)[0] * gain).astype(jnp.bfloat16)
        if i == 0:
            bias[i] = jnp.where(token >= position, 0.0, MASKED)
        elif len(images) == SPAN:
            bias[i] = jnp.where(token < position, 0.0, MASKED)
        else:
            bias[i] = jnp.where(i <= shard, 0.0, MASKED)
    for pair in range(group // 2):
        heads = [2 * pair, 2 * pair + 1]
        q_pair = jnp.concatenate([q_ref[:, g * HD : (g + 1) * HD] for g in heads], 0)
        do_pair = jnp.concatenate([do_ref[:, g * HD : (g + 1) * HD] for g in heads], 0)
        top = None
        for i in images:
            scores = dot(normed[i], q_pair, NT) * (SCALE * LOG2E) + bias[i]
            s_ref[i] = scores
            high = jnp.max(scores, 0, keepdims=True)
            top = high if top is None else jnp.maximum(top, high)
        total = 0.0
        weighted = 0.0
        for i in images:
            value = value_ref[...] if i == 0 else recv[i - 1][:, HD:]
            dprob = dot(value, do_pair, NT)
            weight = jnp.exp2(s_ref[i] - top)
            s_ref[i] = weight
            dp_ref[i] = dprob
            total = total + jnp.sum(weight, 0, keepdims=True)
            weighted = weighted + jnp.sum(weight * dprob, 0, keepdims=True)
        inverse = 1.0 / total
        delta = weighted * inverse
        dq_turned = 0.0
        for i in images:
            prob = s_ref[i] * inverse
            prob_low = prob.astype(jnp.bfloat16)
            dscore = (prob * (dp_ref[i] - delta)).astype(jnp.bfloat16)
            dv = dot(prob_low, do_pair, NN)
            dk = dot(dscore, q_pair, NN)
            if pair == 0:
                dv_ref[i] = dv
                dk_ref[i] = dk
            else:
                dv_ref[i] += dv
                dk_ref[i] += dk
            dq_turned = dq_turned + dot(normed[i], dscore, TN)
        dq = (dq_turned.T * SCALE).astype(jnp.bfloat16)
        for j, g in enumerate(heads):
            dq_ref[:, g * HD : (g + 1) * HD] = dq[j * tokens : (j + 1) * tokens]
    gain_sum = jnp.zeros_like(gain)
    for i in images:
        raw = key_ref[...] if i == 0 else recv[i - 1][:, :HD]
        dk = dk_ref[i] * SCALE
        gain_sum = gain_sum + jnp.sum(dk * unit_norm(raw)[0], 0, keepdims=True)
        if i == 0:
            own_k[...] = dk
            own_v[...] = dv_ref[i]
        else:
            parts[i - 1][:, :HD] = dk.astype(jnp.bfloat16)
            parts[i - 1][:, HD:] = dv_ref[i].astype(jnp.bfloat16)
    gain_part[...] += gain_sum


def attend_kernel(meta, q_ref, do_ref, key_ref, value_ref, *rest, aliased):
    recv, gain_ref, rest = rest[:DOC_IMG], rest[DOC_IMG], rest[DOC_IMG + 1 :]
    if aliased:
        rest = rest[1:]
    dq_ref, own_k, own_v, *rest = rest
    parts, gain_part, scratch = rest[:DOC_IMG], rest[DOC_IMG], rest[DOC_IMG + 1 :]

    @pl.when(pl.program_id(0) == 0)
    def _():
        gain_part[...] = jnp.zeros_like(gain_part)

    args = (
        meta, q_ref, do_ref, key_ref, value_ref, recv, gain_ref,
        dq_ref, own_k, own_v, parts, gain_part, *scratch,
    )

    @pl.when(meta[0] == 0)
    def _():
        head_work(tuple(range(SPAN)), *args)

    @pl.when(meta[0] != 0)
    def _():
        head_work(tuple(range(DOC_IMG)), *args)


def attend(meta, queries, grad_out, key_raw, values, recv, gain, dq, chunk):
    tokens, width = queries.shape
    rows = key_raw.shape[0]
    kv_heads = key_raw.shape[1] // HD
    group = width // HD // kv_heads
    first, heads = sum(HEADS[:chunk]), HEADS[chunk]
    wide = pl.BlockSpec((tokens, group * HD), lambda h: (0, first + h))
    own = pl.BlockSpec((rows, HD), lambda h: (0, first + h))
    part = pl.BlockSpec((rows, 2 * HD), lambda h: (0, h))
    local = pl.BlockSpec((rows, HD), lambda h: (0, h))
    single = pl.BlockSpec((1, HD), lambda h: (0, 0))
    in_specs = [pl.BlockSpec(memory_space=pltpu.SMEM), wide, wide, own, own]
    in_specs += [part] * DOC_IMG + [single]
    args = [meta, queries, grad_out, key_raw, values, *recv, gain]
    aliases = {}
    if dq is not None:
        aliases = {len(args): 0}
        in_specs.append(pl.BlockSpec(memory_space=pl.ANY))
        args.append(dq)
    f32, bf16 = jnp.float32, jnp.bfloat16
    outs = pl.pallas_call(
        functools.partial(attend_kernel, aliased=dq is not None),
        grid=(heads,),
        in_specs=in_specs,
        out_specs=[wide, local, local] + [part] * DOC_IMG + [single],
        out_shape=[jax.ShapeDtypeStruct(queries.shape, bf16)]
        + [jax.ShapeDtypeStruct((rows, heads * HD), f32)] * 2
        + [jax.ShapeDtypeStruct((rows, 2 * heads * HD), bf16)] * DOC_IMG
        + [jax.ShapeDtypeStruct((1, HD), f32)],
        scratch_shapes=[
            pltpu.VMEM((SPAN, rows, 2 * tokens), f32),
            pltpu.VMEM((SPAN, rows, 2 * tokens), f32),
            pltpu.VMEM((SPAN, rows, HD), bf16),
            pltpu.VMEM((SPAN, rows, HD), f32),
            pltpu.VMEM((SPAN, rows, HD), f32),
        ],
        input_output_aliases=aliases,
        compiler_params=pltpu.CompilerParams(vmem_limit_bytes=VMEM_LIMIT),
        cost_estimate=pl.CostEstimate(
            flops=10 * heads * group * tokens * SPAN * rows * HD,
            bytes_accessed=heads * (6 * group * tokens * HD + 24 * SPAN * rows * HD),
            transcendentals=heads * group * tokens * SPAN * rows,
        ),
    )(*args)
    return outs[0], outs[1], outs[2], outs[3 : 3 + DOC_IMG], outs[3 + DOC_IMG]


def finish_kernel(meta, key_ref, own_k, own_v, *rest, aliased):
    back, gain_ref, rest = rest[:DOC_IMG], rest[DOC_IMG], rest[DOC_IMG + 1 :]
    if aliased:
        rest = rest[2:]
    gk_ref, gv_ref = rest
    shard = meta[0]
    unit, inv_rms = unit_norm(key_ref[...])
    dk, dv = own_k[...], own_v[...]
    for distance, ref in enumerate(back, 1):
        dk_part = ref[:, :HD].astype(jnp.float32)
        dv_part = ref[:, HD:].astype(jnp.float32)
        if distance < DOC_IMG:
            held = shard + distance < DOC_IMG
            dk_part = jnp.where(held, dk_part, 0.0)
            dv_part = jnp.where(held, dv_part, 0.0)
        dk = dk + dk_part
        dv = dv + dv_part
    scaled = dk * gain_ref[...]
    inner = jnp.mean(scaled * unit, -1, keepdims=True)
    gk_ref[...] = (inv_rms * (scaled - unit * inner)).astype(gk_ref.dtype)
    gv_ref[...] = dv.astype(gv_ref.dtype)


def finish(meta, key_raw, own_k, own_v, back, gain, done, chunk):
    rows, width = key_raw.shape
    first, heads = sum(HEADS[:chunk]), HEADS[chunk]
    local = pl.BlockSpec((rows, HD), lambda h: (0, h))
    part = pl.BlockSpec((rows, 2 * HD), lambda h: (0, h))
    placed = pl.BlockSpec((rows, HD), lambda h: (0, first + h))
    args = [meta, key_raw, own_k, own_v, *back, gain]
    in_specs = [pl.BlockSpec(memory_space=pltpu.SMEM), placed, local, local]
    in_specs += [part] * DOC_IMG + [pl.BlockSpec((1, HD), lambda h: (0, 0))]
    aliases = {}
    if done is not None:
        aliases = {len(args): 0, len(args) + 1: 1}
        in_specs += [pl.BlockSpec(memory_space=pl.ANY)] * 2
        args += done
    return pl.pallas_call(
        functools.partial(finish_kernel, aliased=done is not None),
        grid=(heads,),
        in_specs=in_specs,
        out_specs=[placed, placed],
        out_shape=[jax.ShapeDtypeStruct(key_raw.shape, jnp.bfloat16)] * 2,
        input_output_aliases=aliases,
        cost_estimate=pl.CostEstimate(
            flops=20 * rows * heads * HD, bytes_accessed=30 * rows * heads * HD, transcendentals=0
        ),
    )(*args)


def reader_pairs(count, distance):
    pairs = []
    for reader in range(distance, count):
        place = reader % DOC_IMG
        if place == 0 or distance <= place:
            pairs.append((reader - distance, reader))
    return pairs


def ring_pairs(count, distance):
    pairs = []
    for reader in range(count):
        place = reader % DOC_IMG
        if place >= distance or (place == 0 and reader):
            pairs.append((reader, reader - place + (place - distance) % DOC_IMG))
    return pairs


def before_pairs(count):
    return [(reader, reader - DOC_IMG) for reader in range(DOC_IMG, count)]


def all_sum(value, axis, steps):
    for step in steps:
        pairs = [(i, i ^ step) for i in range(lax.axis_size(axis))]
        value = value + lax.ppermute(value, axis, pairs)
    return value


def shards(queries, grad_out, key_raw, values, key_gain, image_pos):
    count = lax.axis_size("ctx")
    queries, grad_out = queries[0], grad_out[0]
    key_raw, values = key_raw[0, 0], values[0, 0]
    gain = key_gain[None]
    shard = lax.axis_index("ctx") % DOC_IMG
    meta = jnp.stack([shard, image_pos[0, 0]]).astype(jnp.int32)
    pairs = [reader_pairs(count, distance) for distance in range(1, SPAN)]
    recv = []
    for chunk in range(len(HEADS)):
        packed = pack(key_raw, values, chunk)
        recv.append([lax.ppermute(packed, "ctx", to) for to in pairs])
    dq = done = None
    gain_part = 0.0
    own, back = [], []
    for chunk in range(len(HEADS)):
        dq, own_k, own_v, parts, part = attend(
            meta, queries, grad_out, key_raw, values, recv[chunk], gain, dq, chunk
        )
        gain_part = gain_part + part
        own.append((own_k, own_v))
        back.append(
            [
                lax.ppermute(parts[distance - 1], "ctx", ring_pairs(count, distance))
                for distance in range(1, DOC_IMG)
            ]
        )
        handed = lax.select_n(shard, parts[-1], *back[chunk][::-1])
        if chunk == len(HEADS) - 1:
            gain_part = all_sum(gain_part, "dp", (1, 2, 4))
            gain_part = all_sum(gain_part, "ctx", (4, 8))
            if done is None:
                handed, gain_part = lax.optimization_barrier((handed, gain_part))
            else:
                handed, gain_part, done = lax.optimization_barrier((handed, gain_part, done))
        back[chunk].append(lax.ppermute(handed, "ctx", before_pairs(count)))
        if chunk == len(HEADS) - 1:
            gain_part = all_sum(gain_part, "ctx", (1, 2))
        done = finish(meta, key_raw, *own[chunk], back[chunk], gain, done, chunk)
    return dq[None], done[0][None, None], done[1][None, None], gain_part[0]


def solution(mesh):
    return jax.shard_map(
        shards,
        mesh=mesh,
        in_specs=(
            P("dp", "ctx", None),
            P("dp", "ctx", None),
            P("dp", "ctx", None, None),
            P("dp", "ctx", None, None),
            P(),
            P("dp", "ctx"),
        ),
        out_specs=(
            P("dp", "ctx", None),
            P("dp", "ctx", None, None),
            P("dp", "ctx", None, None),
            P(),
        ),
        check_vma=False,
    )
```

```python
import functools

import jax
import jax.numpy as jnp
from jax import lax
import jax.experimental.pallas as pl
import jax.experimental.pallas.tpu as pltpu
from jax.sharding import PartitionSpec as P

DOC_IMG = 4
SPAN = DOC_IMG + 1
HEADS = (4, 4)
HD = 128
PER = 2
MASKED = -1e30
SCALE = HD**-0.5
LOG2E = 1.4426950408889634
NT = (((1,), (1,)), ((), ()))
TN = (((0,), (0,)), ((), ()))
NN = (((1,), (0,)), ((), ()))
VMEM_LIMIT = 60 * 2**20


def dot(left, right, dims):
    return lax.dot_general(left, right, dims, preferred_element_type=jnp.float32)


def unit_norm(raw):
    wide = raw.astype(jnp.float32)
    inv_rms = lax.rsqrt(jnp.mean(wide * wide, -1, keepdims=True) + 1e-05)
    return wide * inv_rms, inv_rms


def pack_kernel(key_ref, value_ref, out_ref):
    for head in range(key_ref.shape[1] // HD):
        left = 2 * HD * head
        out_ref[:, left : left + HD] = key_ref[:, HD * head : HD * (head + 1)]
        out_ref[:, left + HD : left + 2 * HD] = value_ref[:, HD * head : HD * (head + 1)]


def pack(key_raw, values, chunk):
    rows, width = key_raw.shape
    first, heads = sum(HEADS[:chunk]), HEADS[chunk]
    part = heads * HD
    return pl.pallas_call(
        pack_kernel,
        grid=(heads // 2,),
        in_specs=[pl.BlockSpec((rows, 2 * HD), lambda i: (0, first // 2 + i))] * 2,
        out_specs=pl.BlockSpec((rows, 4 * HD), lambda i: (0, i)),
        out_shape=jax.ShapeDtypeStruct((rows, 2 * part), key_raw.dtype),
        cost_estimate=pl.CostEstimate(flops=0, bytes_accessed=8 * rows * part, transcendentals=0),
    )(key_raw, values)


def head_work(
    first, meta, q_ref, do_ref, key_ref, value_ref, recv, gain_ref,
    dq_ref, own_k, own_v, parts, gain_part, s_ref, dp_ref, normed, both_keys, both_values, dk_ref, dv_ref,
):
    shard, position = meta[0], meta[1]
    gain = gain_ref[...]
    tokens = q_ref.shape[0]
    group = q_ref.shape[1] // HD
    cols = PER * tokens
    token = lax.broadcasted_iota(jnp.int32, (1, cols), 1) % tokens
    images = tuple(range(SPAN if first else DOC_IMG))
    blocks = images[1:] if first else images
    bias = {}
    for i in images:
        raw = key_ref[...] if i == 0 else recv[i - 1][:, :HD]
        keys = (unit_norm(raw)[0] * gain).astype(jnp.bfloat16)
        if first and i in (0, DOC_IMG):
            half = slice(HD, 2 * HD) if i == 0 else slice(0, HD)
            both_keys[:, half] = keys
            both_values[:, half] = value_ref[...] if i == 0 else recv[i - 1][:, HD:]
        else:
            normed[i] = keys
        if first:
            bias[i] = jnp.where(token < position, 0.0, MASKED)
        elif i == 0:
            bias[i] = jnp.where(token >= position, 0.0, MASKED)
        else:
            bias[i] = jnp.where(i <= shard, 0.0, MASKED)
    if first:
        row = lax.broadcasted_iota(jnp.int32, (cols, HD), 0) % tokens
        early = jnp.where(row < position, 1.0, 0.0).astype(jnp.bfloat16)
        late = jnp.where(row >= position, 1.0, 0.0).astype(jnp.bfloat16)
    def load(step):
        heads = [PER * step + j for j in range(PER)]
        q_rows = jnp.concatenate([q_ref[:, g * HD : (g + 1) * HD] for g in heads], 0)
        do_rows = jnp.concatenate([do_ref[:, g * HD : (g + 1) * HD] for g in heads], 0)
        if first:
            q_both = jnp.concatenate([q_rows * early, q_rows * late], 1)
            do_both = jnp.concatenate([do_rows * early, do_rows * late], 1)
        return heads, q_rows, do_rows, q_both if first else None, do_both if first else None

    def scored(step, q_rows, q_both):
        top = None
        for i in blocks:
            if first and i == DOC_IMG:
                scores = dot(both_keys[...], q_both, NT) * (SCALE * LOG2E)
            else:
                scores = dot(normed[i], q_rows, NT) * (SCALE * LOG2E) + bias[i]
            s_ref[step % 2, i] = scores
            high = jnp.max(scores, 0, keepdims=True)
            top = high if top is None else jnp.maximum(top, high)
        return top

    steps = group // PER
    at_hand = load(0)
    top = scored(0, at_hand[1], at_hand[3])
    for step in range(steps):
        heads, q_rows, do_rows, q_both, do_both = at_hand
        total = 0.0
        weighted = 0.0
        for i in blocks:
            if first and i == DOC_IMG:
                dprob = dot(both_values[...], do_both, NT)
            else:
                dprob = dot(value_ref[...] if i == 0 else recv[i - 1][:, HD:], do_rows, NT)
            weight = jnp.exp2(s_ref[step % 2, i] - top)
            s_ref[step % 2, i] = weight
            dp_ref[step % 2, i] = dprob
            total = total + jnp.sum(weight, 0, keepdims=True)
            weighted = weighted + jnp.sum(weight * dprob, 0, keepdims=True)
        inverse = 1.0 / total
        delta = weighted * inverse
        if step + 1 < steps:
            at_hand = load(step + 1)
            top = scored(step + 1, at_hand[1], at_hand[3])
        dq = 0.0
        for i in blocks:
            prob = s_ref[step % 2, i] * inverse
            prob_low = prob.astype(jnp.bfloat16)
            dscore = (prob * (dp_ref[step % 2, i] - delta)).astype(jnp.bfloat16)
            if first and i == DOC_IMG:
                dv = dot(prob_low, do_both, NN)
                dk = dot(dscore, q_both, NN)
                pieces = ((i, dk[:, :HD], dv[:, :HD]), (0, dk[:, HD:], dv[:, HD:]))
                dq_both = dot(both_keys[...], dscore, TN)
                dq = dq + jnp.where(token < position, dq_both[:HD], dq_both[HD:])
            else:
                pieces = ((i, dot(dscore, q_rows, NN), dot(prob_low, do_rows, NN)),)
                dq = dq + dot(normed[i], dscore, TN)
            for image, dk, dv in pieces:
                if step == 0:
                    dk_ref[image] = dk
                    dv_ref[image] = dv
                else:
                    dk_ref[image] += dk
                    dv_ref[image] += dv
        dq = (dq.T * SCALE).astype(jnp.bfloat16)
        for j, g in enumerate(heads):
            dq_ref[:, g * HD : (g + 1) * HD] = dq[j * tokens : (j + 1) * tokens]
    gain_sum = jnp.zeros_like(gain)
    for i in images:
        raw = key_ref[...] if i == 0 else recv[i - 1][:, :HD]
        dk = dk_ref[i] * SCALE
        gain_sum = gain_sum + jnp.sum(dk * unit_norm(raw)[0], 0, keepdims=True)
        if i == 0:
            own_k[...] = dk
            own_v[...] = dv_ref[i]
        else:
            parts[i - 1][:, :HD] = dk.astype(jnp.bfloat16)
            parts[i - 1][:, HD:] = dv_ref[i].astype(jnp.bfloat16)
    gain_part[...] += gain_sum


def attend_kernel(meta, q_ref, do_ref, key_ref, value_ref, *rest, aliased):
    recv, gain_ref, rest = rest[:DOC_IMG], rest[DOC_IMG], rest[DOC_IMG + 1 :]
    if aliased:
        rest = rest[1:]
    dq_ref, own_k, own_v, *rest = rest
    parts, gain_part, scratch = rest[:DOC_IMG], rest[DOC_IMG], rest[DOC_IMG + 1 :]

    @pl.when(pl.program_id(0) == 0)
    def _():
        gain_part[...] = jnp.zeros_like(gain_part)

    args = (
        meta, q_ref, do_ref, key_ref, value_ref, recv, gain_ref,
        dq_ref, own_k, own_v, parts, gain_part, *scratch,
    )

    @pl.when(meta[0] == 0)
    def _():
        head_work(True, *args)

    @pl.when(meta[0] != 0)
    def _():
        head_work(False, *args)


def attend(meta, queries, grad_out, key_raw, values, recv, gain, dq, chunk):
    tokens, width = queries.shape
    rows = key_raw.shape[0]
    kv_heads = key_raw.shape[1] // HD
    group = width // HD // kv_heads
    first, heads = sum(HEADS[:chunk]), HEADS[chunk]
    wide = pl.BlockSpec((tokens, group * HD), lambda h: (0, first + h))
    own = pl.BlockSpec((rows, HD), lambda h: (0, first + h))
    part = pl.BlockSpec((rows, 2 * HD), lambda h: (0, h))
    local = pl.BlockSpec((rows, HD), lambda h: (0, h))
    single = pl.BlockSpec((1, HD), lambda h: (0, 0))
    in_specs = [pl.BlockSpec(memory_space=pltpu.SMEM), wide, wide, own, own]
    in_specs += [part] * DOC_IMG + [single]
    args = [meta, queries, grad_out, key_raw, values, *recv, gain]
    aliases = {}
    if dq is not None:
        aliases = {len(args): 0}
        in_specs.append(pl.BlockSpec(memory_space=pl.ANY))
        args.append(dq)
    f32, bf16 = jnp.float32, jnp.bfloat16
    outs = pl.pallas_call(
        functools.partial(attend_kernel, aliased=dq is not None),
        grid=(heads,),
        in_specs=in_specs,
        out_specs=[wide, local, local] + [part] * DOC_IMG + [single],
        out_shape=[jax.ShapeDtypeStruct(queries.shape, bf16)]
        + [jax.ShapeDtypeStruct((rows, heads * HD), f32)] * 2
        + [jax.ShapeDtypeStruct((rows, 2 * heads * HD), bf16)] * DOC_IMG
        + [jax.ShapeDtypeStruct((1, HD), f32)],
        scratch_shapes=[
            pltpu.VMEM((2, SPAN, rows, PER * tokens), f32),
            pltpu.VMEM((2, SPAN, rows, PER * tokens), f32),
            pltpu.VMEM((SPAN, rows, HD), bf16),
            pltpu.VMEM((rows, 2 * HD), bf16),
            pltpu.VMEM((rows, 2 * HD), bf16),
            pltpu.VMEM((SPAN, rows, HD), f32),
            pltpu.VMEM((SPAN, rows, HD), f32),
        ],
        input_output_aliases=aliases,
        compiler_params=pltpu.CompilerParams(vmem_limit_bytes=VMEM_LIMIT),
        cost_estimate=pl.CostEstimate(
            flops=10 * heads * group * tokens * SPAN * rows * HD,
            bytes_accessed=heads * (6 * group * tokens * HD + 24 * SPAN * rows * HD),
            transcendentals=heads * group * tokens * SPAN * rows,
        ),
    )(*args)
    return outs[0], outs[1], outs[2], outs[3 : 3 + DOC_IMG], outs[3 + DOC_IMG]


def finish_kernel(meta, key_ref, own_k, own_v, *rest, aliased):
    back, gain_ref, rest = rest[:DOC_IMG], rest[DOC_IMG], rest[DOC_IMG + 1 :]
    if aliased:
        rest = rest[2:]
    gk_ref, gv_ref = rest
    shard = meta[0]
    for head in range(key_ref.shape[1] // HD):
        at = slice(head * HD, (head + 1) * HD)
        left = 2 * HD * head
        unit, inv_rms = unit_norm(key_ref[:, at])
        dk, dv = own_k[:, at], own_v[:, at]
        for distance, ref in enumerate(back, 1):
            dk_part = ref[:, left : left + HD].astype(jnp.float32)
            dv_part = ref[:, left + HD : left + 2 * HD].astype(jnp.float32)
            if distance < DOC_IMG:
                held = shard + distance < DOC_IMG
                dk_part = jnp.where(held, dk_part, 0.0)
                dv_part = jnp.where(held, dv_part, 0.0)
            dk = dk + dk_part
            dv = dv + dv_part
        scaled = dk * gain_ref[...]
        inner = jnp.mean(scaled * unit, -1, keepdims=True)
        gk_ref[:, at] = (inv_rms * (scaled - unit * inner)).astype(gk_ref.dtype)
        gv_ref[:, at] = dv.astype(gv_ref.dtype)


def finish(meta, key_raw, own_k, own_v, back, gain, done, chunk):
    rows, width = key_raw.shape
    first, heads = sum(HEADS[:chunk]), HEADS[chunk]
    local = pl.BlockSpec((rows, 2 * HD), lambda h: (0, h))
    part = pl.BlockSpec((rows, 4 * HD), lambda h: (0, h))
    placed = pl.BlockSpec((rows, 2 * HD), lambda h: (0, first // 2 + h))
    args = [meta, key_raw, own_k, own_v, *back, gain]
    in_specs = [pl.BlockSpec(memory_space=pltpu.SMEM), placed, local, local]
    in_specs += [part] * DOC_IMG + [pl.BlockSpec((1, HD), lambda h: (0, 0))]
    aliases = {}
    if done is not None:
        aliases = {len(args): 0, len(args) + 1: 1}
        in_specs += [pl.BlockSpec(memory_space=pl.ANY)] * 2
        args += done
    return pl.pallas_call(
        functools.partial(finish_kernel, aliased=done is not None),
        grid=(heads // 2,),
        in_specs=in_specs,
        out_specs=[placed, placed],
        out_shape=[jax.ShapeDtypeStruct(key_raw.shape, jnp.bfloat16)] * 2,
        input_output_aliases=aliases,
        cost_estimate=pl.CostEstimate(
            flops=20 * rows * heads * HD, bytes_accessed=30 * rows * heads * HD, transcendentals=0
        ),
    )(*args)


def reader_pairs(count, distance):
    pairs = []
    for reader in range(distance, count):
        place = reader % DOC_IMG
        if place == 0 or distance <= place:
            pairs.append((reader - distance, reader))
    return pairs


def ring_pairs(count, distance):
    pairs = []
    for reader in range(count):
        place = reader % DOC_IMG
        if place >= distance or (place == 0 and reader):
            pairs.append((reader, reader - place + (place - distance) % DOC_IMG))
    return pairs


def before_pairs(count):
    return [(reader, reader - DOC_IMG) for reader in range(DOC_IMG, count)]


def all_sum(value, axis, steps):
    for step in steps:
        pairs = [(i, i ^ step) for i in range(lax.axis_size(axis))]
        value = value + lax.ppermute(value, axis, pairs)
    return value


def shards(queries, grad_out, key_raw, values, key_gain, image_pos):
    count = lax.axis_size("ctx")
    queries, grad_out = queries[0], grad_out[0]
    key_raw, values = key_raw[0, 0], values[0, 0]
    gain = key_gain[None]
    shard = lax.axis_index("ctx") % DOC_IMG
    meta = jnp.stack([shard, image_pos[0, 0]]).astype(jnp.int32)
    pairs = [reader_pairs(count, distance) for distance in range(1, SPAN)]
    recv = []
    for chunk in range(len(HEADS)):
        packed = pack(key_raw, values, chunk)
        recv.append([lax.ppermute(packed, "ctx", to) for to in pairs])
    dq = done = None
    gain_part = 0.0
    own, back = [], []
    for chunk in range(len(HEADS)):
        dq, own_k, own_v, parts, part = attend(
            meta, queries, grad_out, key_raw, values, recv[chunk], gain, dq, chunk
        )
        gain_part = gain_part + part
        own.append((own_k, own_v))
        back.append(
            [
                lax.ppermute(parts[distance - 1], "ctx", ring_pairs(count, distance))
                for distance in range(1, DOC_IMG)
            ]
        )
        handed = lax.select_n(shard, parts[-1], *back[chunk][::-1])
        if chunk == len(HEADS) - 1:
            gain_part = all_sum(gain_part, "dp", (1, 2, 4))
            gain_part = all_sum(gain_part, "ctx", (4, 8))
            if done is None:
                handed, gain_part = lax.optimization_barrier((handed, gain_part))
            else:
                handed, gain_part, done = lax.optimization_barrier((handed, gain_part, done))
        back[chunk].append(lax.ppermute(handed, "ctx", before_pairs(count)))
        if chunk == len(HEADS) - 1:
            gain_part = all_sum(gain_part, "ctx", (1, 2))
        done = finish(meta, key_raw, *own[chunk], back[chunk], gain, done, chunk)
    return dq[None], done[0][None, None], done[1][None, None], gain_part[0]


def solution(mesh):
    return jax.shard_map(
        shards,
        mesh=mesh,
        in_specs=(
            P("dp", "ctx", None),
            P("dp", "ctx", None),
            P("dp", "ctx", None, None),
            P("dp", "ctx", None, None),
            P(),
            P("dp", "ctx"),
        ),
        out_specs=(
            P("dp", "ctx", None),
            P("dp", "ctx", None, None),
            P("dp", "ctx", None, None),
            P(),
        ),
        check_vma=False,
    )
```
